512 devices in a mesh: rows: 4 (over y), ctx: 16 (over z), expert: 8 (over x, core).
Axes of the slice: x: 4, y: 4, z: 16, core: 2. Of those that a mesh axis runs over, the one named last changes fastest.
Arguments:
- queries: bfloat16 [32, 24, 128], P('expert', 'rows'), may hold values from -6 to 6
- cache_keys: bfloat16 [32, 4, 2048, 128], P('expert', 'rows', 'ctx'), may hold values from -6 to 6
- cache_values: bfloat16 [32, 4, 2048, 128], P('expert', 'rows', 'ctx'), may hold values from -96 to 96
- residual: bfloat16 [32, 3072], P('expert', 'rows'), may hold values from -1.5 to 1.5
- lengths: int32 [32], P('expert'), may hold values from 1 to 2048, as said below
- expert_ids: int32 [32, 2], P('expert'), may hold values from 0 to 7, all different within a row; in each aligned block of 4 rows (0 to 3, 4 to 7, ...) at most 2 rows name the same one
- router: float32 [3072, 8], replicated, may hold values from -0.109375 to 0.109375
- gate_weight: bfloat16 [8, 3072, 16384], P('expert', None, ('rows', 'ctx')), may hold values from -0.109375 to 0.109375
- up_weight: bfloat16 [8, 3072, 16384], P('expert', None, ('rows', 'ctx')), may hold values from -0.109375 to 0.109375
- down_weight: bfloat16 [8, 16384, 3072], P('expert', ('rows', 'ctx')), may hold values from -0.125 to 0.125
Outputs:
- mixed: bfloat16 [32, 3072], P('expert', ('rows', 'ctx'))
The draws below stay inside these ranges and needn't reach their ends.
Inputs may be any that keep to these rules, and one draw needn't show every extreme that they name: `expert_ids`: within each aligned block of 4 rows (the rows of one device along expert) no expert is named by more than 2 rows, a bound that some block reaches; the two experts of a row differ, and every expert is named somewhere. `lengths`: at least a quarter of the rows have length 2048.
All inputs are finite; a program needn't handle non-finite values.
Results may differ from the reference program's by a relative error of at most 0.0069.
Values may be sent and summed in bfloat16 or wider, within the bound.
No kernel may reach another device: no remote copies, remote signals or barrier semaphores. Data moves between devices by JAX's collectives and lax.ppermute only.
A program may use at most 64 MiB of HBM per device.

```python
import math
import jax
import jax.numpy as jnp
import numpy as np
from jax import lax

D = 3072
HD = 128
QH = 24
KVH = 4
FF = 16384
EXPERTS = 8
TOPK = 2
ITERS = 12
ROWS_DEV = 4
B = 32
CONTEXT = 2048
CAP = 2


def flat_rows(key):
    key = jax.random.fold_in(key, 101)
    pick_key, size_key = jax.random.split(key)
    flat_count = max(B // 4, 1)
    chosen = jax.random.permutation(pick_key, B) < flat_count
    factors = jnp.exp(jax.random.uniform(size_key, (B,), jnp.float32, math.log(0.015), math.log(0.04)))
    return (chosen, factors)


def draw_queries(key, part):
    chosen, factors = flat_rows(key)
    key = jax.random.fold_in(key, 11)
    base = jnp.clip(jax.random.normal(key, (B, QH, HD), jnp.float32), -6.0, 6.0)
    row_scale = jnp.where(chosen, factors, 1.0)
    return (base * row_scale[:, None, None]).astype(jnp.bfloat16)


def draw_cache_values(key, part):
    chosen, factors = flat_rows(key)
    key = jax.random.fold_in(key, 13)
    base = jnp.clip(jax.random.normal(key, (B, KVH, CONTEXT, HD), jnp.float32), -6.0, 6.0)
    row_scale = jnp.where(chosen, 16.0, 1.0)
    return (base * row_scale[:, None, None, None]).astype(jnp.bfloat16)


def draw_lengths(key, part):
    key = jax.random.fold_in(key, 7)
    base_key, full_key = jax.random.split(key)
    random_lengths = jax.random.randint(base_key, (B,), 1, CONTEXT + 1)
    full_rows = jax.random.permutation(full_key, B) < B // 4
    return jnp.where(full_rows, CONTEXT, random_lengths).astype(jnp.int32)


def strengthened(result, key, source, target, parts, factor):
    def block_of(dim):
        return (jnp.arange(result.shape[dim]) // (result.shape[dim] // parts)).reshape((-1,) + (1,) * (result.ndim - 1 - dim))

    one_side = jax.random.permutation(key, parts)[block_of(target)]
    other_side = (block_of(target) + parts // 2) % parts
    return jnp.where((block_of(source) == one_side) | (block_of(source) == other_side), factor * result, result)


def shard_levels(own_key, dims, cuts, low, largest):
    level, own = 1.0, jax.random.fold_in(own_key, 6)
    for axis_at, parts in cuts:
        draws = jnp.exp(jax.random.uniform(jax.random.fold_in(own, axis_at), (parts,), jnp.float32, low / len(cuts), largest / len(cuts)))
        level = level * jnp.repeat(draws, dims[axis_at] // parts).reshape([-1 if axis == axis_at else 1 for axis in range(len(dims))])
    return level


def shared_out(stream_key, own, number, rows, number_of, top, most, lean):
    ranking = jax.random.permutation(stream_key, number_of)
    heavy_load, common = portions_of(number_of, rows * top, most, lean, True), portions_of(number_of, rows * top, most, lean, False)
    places = jnp.arange(number_of)

    def named(tallies, rotation):
        used = int((tallies > 0).sum())
        fixed = max(1, used // 4)
        passed = fixed + (places - fixed + rotation * (used - fixed)) % max(1, number_of - fixed)
        return jnp.zeros((number_of,), jnp.int32).at[ranking[jnp.where(places < fixed, places, passed)]].set(jnp.asarray(tallies, jnp.int32))

    tallies = jnp.where(number % 4 == 0, named(heavy_load, number // 4), named(common, number - number // 4 - 1))
    mixed = jax.random.permutation(jax.random.fold_in(own, 3), number_of)
    giver, receiver = mixed[0:number_of // 2 * 2:2], mixed[1:number_of // 2 * 2:2]
    room = jnp.minimum(tallies[giver] - 1, most - tallies[receiver]) // 2
    room = jnp.where((giver == ranking[0]) | (receiver == ranking[0]) | (tallies[receiver] == 0), 0, jnp.maximum(room, 0))
    passed = jax.random.randint(jax.random.fold_in(own, 4), (number_of // 2,), 0, 1 << 20) % (room + 1)
    tallies = tallies.at[giver].add(-passed).at[receiver].add(passed)
    items = jnp.searchsorted(jnp.cumsum(tallies), jnp.arange(rows * top), side="right").astype(jnp.int32)
    table = items.reshape(top, rows).T
    table = table[jax.random.permutation(jax.random.fold_in(own, 1), rows)]
    rotation = jax.random.randint(jax.random.fold_in(own, 2), (rows, 1), 0, top)
    return jnp.take_along_axis(table, (jnp.arange(top)[None, :] + rotation) % top, axis=1)


def portions_of(amount, total, most, skew, full):
    portions = [(1 << 20) // math.isqrt(rank ** skew) + 1 for rank in range(1, amount + 1)]
    largest = most if full else min(most, max(-(-total // amount), total * portions[0] // sum(portions)))
    least = 1 if total - largest >= amount - 1 else 0
    given, surplus = [largest] + [least] * (amount - 1), total - largest - least * (amount - 1)
    while surplus > 0:
        free = [i for i in range(1, amount) if given[i] < largest] or [i for i in range(1, amount) if given[i] < most]
        whole, remaining = sum([portions[i] for i in free]), surplus
        for i in free:
            extra = min(most - given[i], max(1, remaining * portions[i] // whole), surplus)
            given[i] = given[i] + extra
            surplus = surplus - extra
    return np.array(given)


def scatter_about(rng, shape, spread, bound, pieces=(), held_as=jnp.bfloat16):
    gain = shard_levels(rng, shape, pieces, -0.22, 0.18) if pieces else 1.0
    result = jax.random.normal(rng, shape, jnp.float32) * spread * gain
    return jnp.minimum(jnp.maximum(result, -bound), bound).astype(held_as)


def heavy_noise(own_key, dims, scale, limit, shards, heavy, held_as=jnp.bfloat16):
    array = scale * jax.random.normal(own_key, dims, jnp.float32)
    if shards:
        array = array * shard_levels(own_key, dims, shards, -0.22, 0.18)
    return jnp.clip(strengthened(array, jax.random.fold_in(own_key, 3), *heavy), -limit, limit).astype(held_as)


def setup_inputs(seed: int = 0) -> dict:
    key_list = jax.random.split(jax.random.key(seed), 11)
    queries = draw_queries(jax.random.fold_in(key_list[10], 71), 0)
    cache_keys = scatter_about(key_list[1], (B, KVH, CONTEXT, HD), 1.0, 6.0, ((0, 8), (1, 4), (2, 16)))
    cache_values = draw_cache_values(jax.random.fold_in(key_list[10], 71), 0)
    residual = scatter_about(key_list[3], (B, D), 0.25, 1.5, ((0, 8), (1, 4)))
    lengths = draw_lengths(jax.random.fold_in(key_list[10], 71), 0)
    expert_ids_keys = jax.random.split(jax.random.fold_in(key_list[5], 1), B // ROWS_DEV)
    expert_ids_turns = jax.random.permutation(jax.random.fold_in(key_list[5], 3), B // ROWS_DEV)
    expert_ids = jax.vmap(lambda own, number: shared_out(jax.random.fold_in(key_list[5], 2), own, number, ROWS_DEV, EXPERTS, TOPK, CAP, 2))(expert_ids_keys, expert_ids_turns).reshape((B, TOPK))
    router = scatter_about(key_list[6], (D, EXPERTS), D ** -0.5, 0.109375, (), jnp.float32)
    gate_weight = scatter_about(key_list[7], (EXPERTS, D, FF), D ** -0.5, 0.109375, ((0, 8), (2, 64)))
    up_weight = scatter_about(key_list[8], (EXPERTS, D, FF), D ** -0.5, 0.109375, ((0, 8), (2, 64)))
    down_weight = heavy_noise(key_list[9], (EXPERTS, FF, D), FF ** -0.5, 0.125, ((0, 8), (1, 64)), (1, 2, 64, 4.0))
    return {"queries": queries, "cache_keys": cache_keys, "cache_values": cache_values, "residual": residual, "lengths": lengths, "expert_ids": expert_ids, "router": router, "gate_weight": gate_weight, "up_weight": up_weight, "down_weight": down_weight}


def total_mass(scaled, usable, middle):
    excess = jnp.maximum(scaled - middle, 0.0)
    return lax.optimization_barrier(jnp.sum(jnp.where(usable, excess * excess, 0.0), axis=-1, keepdims=True))

def attend_row(packed):
    query_row, key_row, value_row, length_row = packed
    groups = QH // KVH
    factor = 0.5 / math.sqrt(HD)
    grouped = query_row.astype(jnp.float32).reshape(KVH, groups, HD)
    raw = jnp.einsum('kgd,kcd->kgc', grouped, key_row.astype(jnp.float32))
    scaled = raw * factor
    usable = (jnp.arange(CONTEXT, dtype=jnp.int32) < length_row)[None, None, :]
    top_score = lax.optimization_barrier(jnp.max(jnp.where(usable, scaled, -1e+30), axis=-1, keepdims=True))
    key_count = length_row.astype(jnp.float32)
    low_end = top_score - 1.0
    high_end = top_score - 1.0 / jnp.sqrt(key_count)
    interval = high_end - low_end
    middle = low_end
    total = jnp.ones_like(low_end)
    for round_index in range(ITERS):
        interval = interval / 2.0
        middle = low_end + interval
        total = total_mass(scaled, usable, middle)
        low_end = jnp.where(total >= 1.0, middle, low_end)
    excess = jnp.maximum(scaled - middle, 0.0)
    weights = jnp.where(usable, excess * excess, 0.0).astype(jnp.bfloat16)
    summed = jnp.einsum('kgc,kcd->kgd', weights.astype(jnp.float32), value_row.astype(jnp.float32))
    return (summed / total).reshape(QH * HD)

def expert_output(hidden, gate_one, up_one, down_one):
    hidden_wide = hidden.astype(jnp.float32)
    gate_act = jnp.dot(hidden_wide, gate_one.astype(jnp.float32), preferred_element_type=jnp.float32)
    up_act = jnp.dot(hidden_wide, up_one.astype(jnp.float32), preferred_element_type=jnp.float32)
    activation = (jax.nn.silu(gate_act) * up_act).astype(jnp.bfloat16)
    return jnp.dot(activation.astype(jnp.float32), down_one.astype(jnp.float32), preferred_element_type=jnp.float32)

def reference(queries, cache_keys, cache_values, residual, lengths, expert_ids, router, gate_weight, up_weight, down_weight):
    attended = lax.map(attend_row, (queries, cache_keys, cache_values, lengths))
    hidden = (residual.astype(jnp.float32) + attended).astype(jnp.bfloat16)
    logits = jnp.dot(hidden.astype(jnp.float32), router, precision=lax.Precision.HIGHEST)
    expert_iota = jnp.arange(EXPERTS, dtype=jnp.int32)
    picked = expert_ids[:, :, None] == expert_iota[None, None, :]
    chosen = lax.optimization_barrier(jnp.sum(jnp.where(picked, logits[:, None, :], 0.0), axis=-1))
    first_share = 1.0 / (1.0 + jnp.exp(chosen[:, 1] - chosen[:, 0]))
    second_share = 1.0 / (1.0 + jnp.exp(chosen[:, 0] - chosen[:, 1]))
    shares = jnp.stack([first_share, second_share], axis=1)
    expert_shares = lax.optimization_barrier(jnp.sum(jnp.where(picked, shares[:, :, None], 0.0), axis=1))

    def add_expert(running, packed):
        gate_one, up_one, down_one, share_column = packed
        expert_out = expert_output(hidden, gate_one, up_one, down_one)
        return (running + share_column[:, None] * expert_out, None)
    start_total = jnp.zeros((B, D), jnp.float32)
    combined, unused = lax.scan(add_expert, start_total, (gate_weight, up_weight, down_weight, expert_shares.T))
    return (hidden.astype(jnp.float32) + combined).astype(jnp.bfloat16)
```

```python
import functools
import math

import jax
import jax.numpy as jnp
from jax import lax
from jax.experimental import pallas as pl
from jax.experimental.pallas import tpu as pltpu
from jax.sharding import PartitionSpec as P

ITERS = 12
VMEM = pl.BlockSpec(memory_space=pltpu.VMEM)
SMEM = pl.BlockSpec(memory_space=pltpu.SMEM)
F32 = jnp.float32
BF16 = jnp.bfloat16
NEG = -1e30
HBM = pl.BlockSpec(memory_space=pltpu.HBM)
NT = (((1,), (1,)), ((), ()))


def call(kernel, outs, *args, specs, out_spec=VMEM, scratch=(), limit=16 << 20):
    return pl.pallas_call(
        kernel,
        out_shape=outs,
        in_specs=specs,
        out_specs=jax.tree.map(lambda _: out_spec, outs),
        scratch_shapes=scratch,
        compiler_params=pltpu.CompilerParams(vmem_limit_bytes=limit),
        cost_estimate=pl.CostEstimate(flops=1 << 36, bytes_accessed=1 << 28, transcendentals=0),
    )(*args)


def iota(shape, dim):
    return lax.broadcasted_iota(jnp.int32, shape, dim)


def one_hot(mask):
    return jnp.where(mask, 1.0, 0.0).astype(BF16)


def parts_of(x, count):
    parts = []
    for _ in range(count):
        part = x.astype(BF16)
        parts.append(part)
        x = x - part.astype(F32)
    return parts


def score_kernel(
    heads, k_hbm, q_hbm, len_hbm, res_hbm, v_hbm, out_hbm, out_ref, k_ref, q_ref, len_ref, res_ref, v_ref, sems, out_sems
):
    pairs = ((k_hbm, k_ref), (q_hbm, q_ref), (len_hbm, len_ref), (res_hbm, res_ref), (v_hbm, v_ref))
    copies = [pltpu.make_async_copy(src, dst, sems.at[i]) for i, (src, dst) in enumerate(pairs)]
    for copy in copies:
        copy.start()
    n_b, here, size = k_ref.shape
    split = out_ref.shape[0] // n_b
    dims = size // split
    c = lax.axis_index("ctx")
    place = c * here + iota((8, here), 1)
    eye = one_hot(iota((size, size), 0) == iota((size, size), 1))
    diagonal = iota((8, here), 0) == iota((8, here), 1)
    head = iota((8, heads * n_b), 0)
    for copy in copies[:4]:
        copy.wait()
    q = q_ref[...]
    res = res_ref[...].astype(F32)
    odd = lax.rem(c, 2) == 1
    half = heads // 2
    tails = []
    for b in range(n_b):
        pick = one_hot((iota(head.shape, 1) == head * n_b + b) & (head < heads))
        q_b = jnp.dot(pick, q, preferred_element_type=F32).astype(BF16)
        scaled = lax.dot_general(q_b, k_ref[b], NT, preferred_element_type=F32) * (0.5 / math.sqrt(size))
        valid = place < len_ref[b]
        top = jnp.max(jnp.where(valid, scaled, NEG), axis=-1, keepdims=True)
        top = jnp.where(top > 0.5 * NEG, top.astype(BF16).astype(F32), 0.0)
        rows = [part.astype(F32)[0:heads] for part in parts_of(jnp.where(valid, scaled - top, NEG), 2)]
        rows.append(jnp.sum(jnp.where(diagonal, top, 0.0), axis=0, keepdims=True))
        for k in range(half):
            even_part, odd_part = (res[b:b + 1, h * size:(h + 1) * size] for h in (k, half + k))
            rows.append(jnp.where(odd, odd_part, even_part))
        tails.append(jnp.concatenate(rows, axis=0))
    copies[4].wait()
    out_copies = []
    for b in range(n_b):
        turned = lax.dot_general(eye, v_ref[b], NT, preferred_element_type=F32)
        for j in range(split):
            block = jnp.concatenate([turned[j * dims:(j + 1) * dims], tails[b]], axis=0)
            out_ref[b * split + j] = block.astype(BF16)
        cut = pl.ds(b * split, split)
        out_copies.append(pltpu.make_async_copy(out_ref.at[cut], out_hbm.at[cut], out_sems.at[b]))
        out_copies[b].start()
    for copy in out_copies:
        copy.wait()


def attend_kernel(heads, split, got_ref, out_ref):
    n_c, rows, here = got_ref.shape
    dims = rows - 16
    j = lax.axis_index("ctx") % split
    parts = got_ref[:, dims:].astype(F32)
    diagonal = iota((n_c, 8, here), 1) == iota((n_c, 8, here), 2)
    tops = jnp.sum(jnp.where(diagonal, parts[:, 2 * heads:2 * heads + 1], 0.0), axis=-1, keepdims=True)
    blank = jnp.full((8 - heads, here), NEG, F32)
    scores = [jnp.concatenate([parts[i, 0:heads] + parts[i, heads:2 * heads], blank], axis=0) for i in range(n_c)]
    scores = jnp.stack(scores) + tops
    count = jnp.sum(jnp.sum(jnp.where(scores > 0.5 * NEG, 1.0, 0.0), axis=0), axis=-1, keepdims=True)
    count = jnp.maximum(count, 1.0)
    top = jnp.max(jnp.max(scores, axis=0), axis=-1, keepdims=True)
    low = top - 1.0
    interval = (top - 1.0 / jnp.sqrt(count)) - low

    def mass(middle):
        excess = jnp.maximum(scores - middle[None], 0.0)
        return jnp.sum(jnp.sum(excess * excess, axis=0), axis=-1, keepdims=True)

    for _ in range(ITERS // 3):
        w1 = interval / 2.0
        w2 = w1 / 2.0
        w3 = w2 / 2.0
        m1 = low + w1
        m2 = (low + w2, m1 + w2)
        m3 = (low + w3, m2[0] + w3, m1 + w3, m2[1] + w3)
        t1, t2, t3 = mass(m1), [mass(m) for m in m2], [mass(m) for m in m3]
        c1 = t1 >= 1.0
        low = jnp.where(c1, m1, low)
        c2 = jnp.where(c1, t2[1], t2[0]) >= 1.0
        low = jnp.where(c2, jnp.where(c1, m2[1], m2[0]), low)
        middle = jnp.where(c1, jnp.where(c2, m3[3], m3[2]), jnp.where(c2, m3[1], m3[0]))
        total = jnp.where(c1, jnp.where(c2, t3[3], t3[2]), jnp.where(c2, t3[1], t3[0]))
        low = jnp.where(total >= 1.0, middle, low)
        interval = w3
    excess = jnp.maximum(scores - middle[None], 0.0)
    weights = excess * excess
    weights = jnp.concatenate([weights[i] for i in range(n_c)], axis=1).astype(BF16)
    values = jnp.concatenate([got_ref[i, 0:dims] for i in range(n_c)], axis=1)
    attended = lax.dot_general(weights, values, NT, preferred_element_type=F32) / total
    attended = jnp.concatenate([attended] * split, axis=1)
    res = [parts[i, 2 * heads + 1:] for i in range(2)]
    res = jnp.concatenate(res + [jnp.zeros((8 - heads, here), F32)], axis=0)
    mine = (iota(res.shape, 1) // dims == j) & (iota(res.shape, 0) < heads)
    piece = jnp.where(mine, res + attended, 0.0).astype(BF16)
    for i in range(n_c):
        out_ref[i] = piece


def hidden_kernel(got_ref, hid_ref, out_ref):
    n_c = got_ref.shape[0]
    rows, size = hid_ref.shape
    n_b = 4
    split = n_c // n_b
    got = got_ref[...].astype(F32)
    whole = []
    for b in range(n_b):
        row = got[b * split]
        for j in range(1, split):
            row = row + got[b * split + j]
        whole.append(row)
    whole = jnp.concatenate(whole, axis=0).astype(BF16)
    at, src = iota((rows, 8 * n_b), 0), iota((rows, 8 * n_b), 1)
    pick = one_hot(src == (at % n_b) * 8 + at // n_b)
    hidden = jnp.dot(pick, whole, preferred_element_type=F32).astype(BF16)
    hid_ref[...] = hidden
    for i in range(out_ref.shape[0]):
        out_ref[i] = hidden


def expert_kernel(
    ids_ref, g_ref, router_ref, gate_ref, up_ref, down_ref, out_ref, share_ref, wide_ref
):
    n_r, n_e, block, _ = out_ref.shape
    n_b = 4
    rows = n_e * n_b
    heads = block // n_b
    width = heads * 128
    at, src = iota((heads * rows, n_e * block), 0), iota((heads * rows, n_e * block), 1)
    inner = at % rows
    pick = one_hot(src == (inner // n_b) * block + (at // rows) * n_b + inner % n_b)
    own = one_hot(iota((block, rows), 1) == lax.axis_index("expert") * n_b + iota((block, rows), 0) % n_b)
    routers = parts_of(router_ref[...], 3)
    gate = up = logits = None
    for r in range(n_r):
        moved = jnp.dot(pick, g_ref[r], preferred_element_type=F32).astype(BF16)
        x = jnp.concatenate([moved[h * rows:(h + 1) * rows] for h in range(heads)], axis=1)
        cols = slice(r * width, (r + 1) * width)
        g = jnp.dot(x, gate_ref[cols], preferred_element_type=F32)
        u = jnp.dot(x, up_ref[cols], preferred_element_type=F32)
        x_own = jnp.dot(own, x, preferred_element_type=F32).astype(BF16)
        hi, mid, low = [lax.dot_general(x_own, m[:, cols], NT, preferred_element_type=F32) for m in routers]
        l = (low + mid) + hi
        gate, up, logits = (g, u, l) if r == 0 else (gate + g, up + u, logits + l)
    act = ((gate / (1.0 + jnp.exp(-gate))) * up).astype(BF16)
    for r in range(n_r):
        o = jnp.dot(act, down_ref[:, r * width:(r + 1) * width], preferred_element_type=F32)
        for h in range(heads):
            piece = o[:, h * 128:(h + 1) * 128]
            for e in range(n_e):
                wide_ref[r, e, h * n_b:(h + 1) * n_b, :] = piece[e * n_b:(e + 1) * n_b]
    out_ref[...] = wide_ref[...].astype(BF16)
    which = iota(logits.shape, 1)
    owner = iota(logits.shape, 0) % n_b
    first = second = jnp.zeros(logits.shape, jnp.int32)
    for b in range(n_b):
        first = jnp.where(owner == b, ids_ref[0, b], first)
        second = jnp.where(owner == b, ids_ref[1, b], second)
    l0 = jnp.sum(jnp.where(which == first, logits, 0.0), axis=-1, keepdims=True)
    l1 = jnp.sum(jnp.where(which == second, logits, 0.0), axis=-1, keepdims=True)
    s0 = 1.0 / (1.0 + jnp.exp(l1 - l0))
    s1 = 1.0 / (1.0 + jnp.exp(l0 - l1))
    share_ref[...] = jnp.where(which == first, s0, 0.0) + jnp.where(which == second, s1, 0.0)


def split_kernel(width, parts_ref, share_ref, hid_ref, out_ref):
    n_c, n_b, _ = out_ref.shape
    n_e = share_ref.shape[1]
    n_r = parts_ref.shape[0] // n_e
    total = None
    for e in range(n_e):
        part = parts_ref[e].astype(F32)
        for r in range(1, n_r):
            part = part + parts_ref[r * n_e + e].astype(F32)
        part = part * share_ref[:, e:e + 1]
        total = part if total is None else total + part
    c = lax.axis_index("ctx")
    col = (iota(total.shape, 0) // n_b) * 128 + iota(total.shape, 1)
    mine = (col >= c * width) & (col < (c + 1) * width)
    total = total + jnp.where(mine, hid_ref[...].astype(F32), 0.0)
    for i in range(n_c):
        h, off = divmod(i * width, 128)
        n = min(width, 128 - off)
        out_ref[i, :, 0:n] = total[h * n_b:(h + 1) * n_b, off:off + n]
        if n < width:
            out_ref[i, :, n:width] = total[(h + 1) * n_b:(h + 2) * n_b, 0:width - n]


def sum_kernel(parts_ref, out_ref):
    total = jnp.sum(parts_ref[...], axis=0)
    out_ref[...] = total[:, 0:out_ref.shape[1]].astype(BF16)


def body(
    queries,
    cache_keys,
    cache_values,
    residual,
    lengths,
    expert_ids,
    router,
    gate_weight,
    up_weight,
    down_weight,
):
    n_b, n_h, size = queries.shape
    here = cache_keys.shape[2]
    n_c, n_r, n_e = (lax.axis_size(a) for a in ("ctx", "rows", "expert"))
    rows = n_b * n_h
    struct = jax.ShapeDtypeStruct
    q = queries.transpose(1, 0, 2).reshape(rows, size)
    keys = cache_keys.reshape(n_b, here, size)
    values = cache_values.reshape(n_b, here, size)

    def swap(x, axes):
        return lax.all_to_all(x, axes, split_axis=0, concat_axis=0, tiled=True)

    dims = size * n_b // n_c
    sent = call(
        functools.partial(score_kernel, n_h), struct((n_c, dims + 16, here), BF16),
        keys, q, lengths, residual, values, specs=[HBM] * 5, out_spec=HBM,
        scratch=[
            pltpu.VMEM((n_c, dims + 16, here), BF16), pltpu.VMEM(keys.shape, BF16), pltpu.VMEM(q.shape, BF16),
            pltpu.SMEM((n_b,), jnp.int32), pltpu.VMEM(residual.shape, BF16), pltpu.VMEM(values.shape, BF16),
            pltpu.SemaphoreType.DMA((5,)), pltpu.SemaphoreType.DMA((n_b,)),
        ],
        limit=60 << 20,
    )
    got = swap(sent, "ctx")
    sent = call(
        functools.partial(attend_kernel, n_h, n_c // n_b), struct((n_c, 8, size), BF16), got, specs=[VMEM],
    )
    got = swap(sent, "ctx")
    hidden, sent = call(
        hidden_kernel, (struct((rows, size), BF16), struct((n_r * n_e, rows, size), BF16)), got, specs=[VMEM],
    )
    got = swap(sent, ("rows", "expert")).reshape(n_r, n_e * rows, size)
    sent, share = call(
        expert_kernel, (struct((n_r, n_e, rows, size), BF16), struct((rows, n_e), F32)),
        expert_ids.T, got, router.T, gate_weight[0], up_weight[0], down_weight[0],
        specs=[SMEM, VMEM, VMEM, VMEM, VMEM, VMEM],
        scratch=[
            pltpu.VMEM((n_r, n_e, rows, size), F32)],
    )
    got = swap(sent.reshape(n_r * n_e, rows, size), ("rows", "expert"))
    width = n_h * size // n_c
    sent = call(
        functools.partial(split_kernel, width), struct((n_c, n_b, 128), F32),
        got, share, hidden, specs=[VMEM, VMEM, VMEM],
    )
    return call(sum_kernel, struct((n_b, width), BF16), swap(sent, "ctx"), specs=[VMEM])


def solution(mesh):
    placed = (
        P("expert", "rows", None),
        P("expert", "rows", "ctx", None),
        P("expert", "rows", "ctx", None),
        P("expert", "rows"),
        P("expert"),
        P("expert", None),
        P(),
        P("expert", None, ("rows", "ctx")),
        P("expert", None, ("rows", "ctx")),
        P("expert", ("rows", "ctx"), None),
    )
    return jax.shard_map(
        body, mesh=mesh, in_specs=placed, out_specs=P("expert", ("rows", "ctx")), check_vma=False
    )
```

```python
import functools
import math

import jax
import jax.numpy as jnp
from jax import lax
from jax.experimental import pallas as pl
from jax.experimental.pallas import tpu as pltpu
from jax.sharding import PartitionSpec as P

ITERS = 12
VMEM = pl.BlockSpec(memory_space=pltpu.VMEM)
SMEM = pl.BlockSpec(memory_space=pltpu.SMEM)
F32 = jnp.float32
BF16 = jnp.bfloat16
NEG = -1e30
HBM = pl.BlockSpec(memory_space=pltpu.HBM)
NT = (((1,), (1,)), ((), ()))


def call(kernel, outs, *args, specs, out_spec=VMEM, scratch=(), limit=16 << 20):
    return pl.pallas_call(
        kernel,
        out_shape=outs,
        in_specs=specs,
        out_specs=jax.tree.map(lambda _: out_spec, outs),
        scratch_shapes=scratch,
        compiler_params=pltpu.CompilerParams(vmem_limit_bytes=limit),
        cost_estimate=pl.CostEstimate(flops=1 << 36, bytes_accessed=1 << 28, transcendentals=0),
    )(*args)


def iota(shape, dim):
    return lax.broadcasted_iota(jnp.int32, shape, dim)


def one_hot(mask):
    return jnp.where(mask, 1.0, 0.0).astype(BF16)


def parts_of(x, count):
    parts = []
    for _ in range(count):
        part = x.astype(BF16)
        parts.append(part)
        x = x - part.astype(F32)
    return parts


def score_kernel(
    heads, k_hbm, q_hbm, len_hbm, res_hbm, v_hbm, out_hbm, out_ref, k_ref, q_ref, len_ref, res_ref, v_ref, sems, out_sems
):
    pairs = ((k_hbm, k_ref), (q_hbm, q_ref), (len_hbm, len_ref), (res_hbm, res_ref), (v_hbm, v_ref))
    copies = [pltpu.make_async_copy(src, dst, sems.at[i]) for i, (src, dst) in enumerate(pairs)]
    for copy in copies:
        copy.start()
    n_b, here, size = k_ref.shape
    split = out_ref.shape[0] // n_b
    dims = size // split
    c = lax.axis_index("ctx")
    place = c * here + iota((8, here), 1)
    eye = one_hot(iota((size, size), 0) == iota((size, size), 1))
    diagonal = iota((8, here), 0) == iota((8, here), 1)
    at, src = iota((8 * n_b, heads * n_b), 0), iota((8 * n_b, heads * n_b), 1)
    pick = one_hot(src == at % 8 * n_b + at // 8)
    for copy in copies[:4]:
        copy.wait()
    q = jnp.dot(pick, q_ref[...], preferred_element_type=F32)
    res = res_ref[...].astype(F32)
    odd = lax.rem(c, 2) == 1
    half = heads // 2
    tails = []
    for b in range(n_b):
        q_b = q[8 * b:8 * b + 8].astype(BF16)
        scaled = lax.dot_general(q_b, k_ref[b], NT, preferred_element_type=F32) * (0.5 / math.sqrt(size))
        valid = place < len_ref[b]
        top = jnp.max(jnp.where(valid, scaled, NEG), axis=-1, keepdims=True)
        top = jnp.where(top > 0.5 * NEG, top.astype(BF16).astype(F32), 0.0)
        rows = [part.astype(F32)[0:heads] for part in parts_of(jnp.where(valid, scaled - top, NEG), 2)]
        rows.append(jnp.sum(jnp.where(diagonal, top, 0.0), axis=0, keepdims=True))
        for k in range(half):
            even_part, odd_part = (res[b:b + 1, h * size:(h + 1) * size] for h in (k, half + k))
            rows.append(jnp.where(odd, odd_part, even_part))
        tails.append(jnp.concatenate(rows, axis=0))
    copies[4].wait()
    out_copies = []
    for b in range(n_b):
        turned = lax.dot_general(eye, v_ref[b], NT, preferred_element_type=F32)
        for j in range(split):
            block = jnp.concatenate([turned[j * dims:(j + 1) * dims], tails[b]], axis=0)
            out_ref[b * split + j] = block.astype(BF16)
        cut = pl.ds(b * split, split)
        out_copies.append(pltpu.make_async_copy(out_ref.at[cut], out_hbm.at[cut], out_sems.at[b]))
        out_copies[b].start()
    for copy in out_copies:
        copy.wait()


def attend_kernel(heads, split, got_ref, out_ref):
    n_c, rows, here = got_ref.shape
    dims = rows - 16
    j = lax.axis_index("ctx") % split
    parts = got_ref[:, dims:].astype(F32)
    diagonal = iota((n_c, 8, here), 1) == iota((n_c, 8, here), 2)
    tops = jnp.sum(jnp.where(diagonal, parts[:, 2 * heads:2 * heads + 1], 0.0), axis=-1, keepdims=True)
    blank = jnp.full((8 - heads, here), NEG, F32)
    scores = [jnp.concatenate([parts[i, 0:heads] + parts[i, heads:2 * heads], blank], axis=0) for i in range(n_c)]
    scores = jnp.stack(scores) + tops
    count = jnp.sum(jnp.sum(jnp.where(scores > 0.5 * NEG, 1.0, 0.0), axis=0), axis=-1, keepdims=True)
    count = jnp.maximum(count, 1.0)
    top = jnp.max(jnp.max(scores, axis=0), axis=-1, keepdims=True)
    low = top - 1.0
    interval = (top - 1.0 / jnp.sqrt(count)) - low

    def mass(middle):
        excess = jnp.maximum(scores - middle[None], 0.0)
        return jnp.sum(jnp.sum(excess * excess, axis=0), axis=-1, keepdims=True)

    for _ in range(ITERS // 3):
        w1 = interval / 2.0
        w2 = w1 / 2.0
        w3 = w2 / 2.0
        m1 = low + w1
        m2 = (low + w2, m1 + w2)
        m3 = (low + w3, m2[0] + w3, m1 + w3, m2[1] + w3)
        t1, t2, t3 = mass(m1), [mass(m) for m in m2], [mass(m) for m in m3]
        c1 = t1 >= 1.0
        low = jnp.where(c1, m1, low)
        c2 = jnp.where(c1, t2[1], t2[0]) >= 1.0
        low = jnp.where(c2, jnp.where(c1, m2[1], m2[0]), low)
        middle = jnp.where(c1, jnp.where(c2, m3[3], m3[2]), jnp.where(c2, m3[1], m3[0]))
        total = jnp.where(c1, jnp.where(c2, t3[3], t3[2]), jnp.where(c2, t3[1], t3[0]))
        low = jnp.where(total >= 1.0, middle, low)
        interval = w3
    excess = jnp.maximum(scores - middle[None], 0.0)
    weights = excess * excess
    weights = jnp.concatenate([weights[i] for i in range(n_c)], axis=1).astype(BF16)
    values = jnp.concatenate([got_ref[i, 0:dims] for i in range(n_c)], axis=1)
    attended = lax.dot_general(weights, values, NT, preferred_element_type=F32) / total
    res = jnp.concatenate([parts[i, 2 * heads + 1:] for i in range(2)] + [jnp.zeros((8 - heads, here), F32)], axis=0)
    mine = res[:, 0:dims]
    for k in range(1, split):
        mine = jnp.where(j == k, res[:, k * dims:(k + 1) * dims], mine)
    hidden = mine + attended
    flat = [hidden[h:h + 1] for h in range(heads)]
    flat += [jnp.zeros((1, dims), F32)] * (-heads % split)
    lines = [jnp.concatenate(flat[h:h + split], axis=1) for h in range(0, len(flat), split)]
    piece = jnp.concatenate(lines, axis=0).astype(BF16)
    for i in range(n_c):
        out_ref[i] = piece


def hidden_kernel(got_ref, hid_ref, out_ref):
    n_c = got_ref.shape[0]
    rows, size = hid_ref.shape
    n_b = 4
    split = n_c // n_b
    dims = size // split
    at, src = iota((n_c, n_c), 0), iota((n_c, n_c), 1)
    pick = one_hot(src == (at % n_b) * split + at // n_b)
    got = got_ref[...].astype(F32)
    moved = [
        jnp.dot(pick, got[:, k].astype(BF16), preferred_element_type=F32) for k in range(got_ref.shape[1])
    ]
    pieces = []
    for h in range(rows // n_b):
        lanes = slice(h % split * dims, (h % split + 1) * dims)
        from_j = [moved[h // split][j * n_b:(j + 1) * n_b, lanes] for j in range(split)]
        pieces.append(jnp.concatenate(from_j, axis=1))
    hidden = jnp.concatenate(pieces, axis=0).astype(BF16)
    hid_ref[...] = hidden
    for i in range(out_ref.shape[0]):
        out_ref[i] = hidden


def expert_kernel(
    ids_ref, g_ref, router_ref, gate_ref, up_ref, down_ref, out_ref, share_ref, logit_ref
):
    n_r, n_e, block, _ = out_ref.shape
    n_b = 4
    rows = n_e * n_b
    heads = block // n_b
    width = heads * 128
    at, src = iota((heads * rows, n_e * block), 0), iota((heads * rows, n_e * block), 1)
    inner = at % rows
    pick = one_hot(src == (inner // n_b) * block + (at // rows) * n_b + inner % n_b)
    at, src = iota((n_e * block, heads * rows), 0), iota((n_e * block, heads * rows), 1)
    inner = at % block
    back = one_hot(src == inner // n_b * rows + at // block * n_b + inner % n_b)
    router = jnp.concatenate([part.astype(F32) for part in parts_of(router_ref[...], 3)], axis=0).astype(BF16)
    gate = up = logits = None
    for r in range(n_r):
        moved = jnp.dot(pick, g_ref[r], preferred_element_type=F32).astype(BF16)
        x = jnp.concatenate([moved[h * rows:(h + 1) * rows] for h in range(heads)], axis=1)
        cols = slice(r * width, (r + 1) * width)
        g = jnp.dot(x, gate_ref[cols], preferred_element_type=F32)
        u = jnp.dot(x, up_ref[cols], preferred_element_type=F32)
        l = lax.dot_general(x, router[:, cols], NT, preferred_element_type=F32)
        gate, up, logits = (g, u, l) if r == 0 else (gate + g, up + u, logits + l)
    act = ((gate / (1.0 + jnp.exp(-gate))) * up).astype(BF16)
    for r in range(n_r):
        o = jnp.dot(act, down_ref[:, r * width:(r + 1) * width], preferred_element_type=F32).astype(BF16)
        o = jnp.concatenate([o[:, h * 128:(h + 1) * 128] for h in range(heads)], axis=0)
        o = jnp.dot(back, o, preferred_element_type=F32)
        for e in range(n_e):
            out_ref[r, e] = o[e * block:(e + 1) * block].astype(BF16)
    logit_ref[...] = (logits[:, 2 * n_e:3 * n_e] + logits[:, n_e:2 * n_e]) + logits[:, 0:n_e]
    logits = logit_ref[pl.ds(lax.axis_index("expert") * n_b, n_b), :]
    logits = jnp.concatenate([logits] * heads, axis=0)
    which = iota(logits.shape, 1)
    owner = iota(logits.shape, 0) % n_b
    first = second = jnp.zeros(logits.shape, jnp.int32)
    for b in range(n_b):
        first = jnp.where(owner == b, ids_ref[0:1, b:b + 1], first)
        second = jnp.where(owner == b, ids_ref[1:2, b:b + 1], second)
    l0 = jnp.sum(jnp.where(which == first, logits, 0.0), axis=-1, keepdims=True)
    l1 = jnp.sum(jnp.where(which == second, logits, 0.0), axis=-1, keepdims=True)
    s0 = 1.0 / (1.0 + jnp.exp(l1 - l0))
    s1 = 1.0 / (1.0 + jnp.exp(l0 - l1))
    share_ref[...] = jnp.where(which == first, s0, 0.0) + jnp.where(which == second, s1, 0.0)


def split_kernel(width, parts_ref, share_ref, hid_ref, out_ref):
    n_c, n_b = out_ref.shape[0], 4
    n_e = share_ref.shape[1]
    n_r = parts_ref.shape[0] // n_e
    total = None
    for e in range(n_e):
        part = parts_ref[e].astype(F32)
        for r in range(1, n_r):
            part = part + parts_ref[r * n_e + e].astype(F32)
        part = part * share_ref[:, e:e + 1]
        total = part if total is None else total + part
    c = lax.axis_index("ctx")
    col = (iota(total.shape, 0) // n_b) * 128 + iota(total.shape, 1)
    mine = (col >= c * width) & (col < (c + 1) * width)
    total = total + jnp.where(mine, hid_ref[...].astype(F32), 0.0)
    for i in range(n_c):
        h, off = divmod(i * width, 128)
        n = min(width, 128 - off)
        out_ref[i, :, 0:n] = total[h * n_b:(h + 1) * n_b, off:off + n]
        if n < width:
            out_ref[i, :, n:width] = total[(h + 1) * n_b:(h + 2) * n_b, 0:width - n]


def sum_kernel(parts_ref, out_ref):
    total = jnp.sum(parts_ref[...], axis=0)
    out_ref[...] = total[:, 0:out_ref.shape[1]].astype(BF16)


def body(
    queries,
    cache_keys,
    cache_values,
    residual,
    lengths,
    expert_ids,
    router,
    gate_weight,
    up_weight,
    down_weight,
):
    n_b, n_h, size = queries.shape
    here = cache_keys.shape[2]
    n_c, n_r, n_e = (lax.axis_size(a) for a in ("ctx", "rows", "expert"))
    rows = n_b * n_h
    struct = jax.ShapeDtypeStruct
    q = queries.transpose(1, 0, 2).reshape(rows, size)
    keys = cache_keys.reshape(n_b, here, size)
    values = cache_values.reshape(n_b, here, size)

    def swap(x, axes):
        return lax.all_to_all(x, axes, split_axis=0, concat_axis=0, tiled=True)

    dims = size * n_b // n_c
    sent = call(
        functools.partial(score_kernel, n_h), struct((n_c, dims + 16, here), BF16),
        keys, q, lengths, residual, values, specs=[HBM] * 5, out_spec=HBM,
        scratch=[
            pltpu.VMEM((n_c, dims + 16, here), BF16), pltpu.VMEM(keys.shape, BF16), pltpu.VMEM(q.shape, BF16),
            pltpu.SMEM((n_b,), jnp.int32), pltpu.VMEM(residual.shape, BF16), pltpu.VMEM(values.shape, BF16),
            pltpu.SemaphoreType.DMA((5,)), pltpu.SemaphoreType.DMA((n_b,)),
        ],
        limit=60 << 20,
    )
    got = swap(sent, "ctx")
    sent = call(
        functools.partial(attend_kernel, n_h, n_c // n_b), struct((n_c, -(-n_h * n_b // n_c), size), BF16), got, specs=[VMEM],
    )
    got = swap(sent, "ctx")
    hidden, sent = call(
        hidden_kernel, (struct((rows, size), BF16), struct((n_r * n_e, rows, size), BF16)), got, specs=[VMEM],
    )
    got = swap(sent, ("rows", "expert")).reshape(n_r, n_e * rows, size)
    sent, share = call(
        expert_kernel, (struct((n_r, n_e, rows, size), BF16), struct((rows, n_e), F32)),
        expert_ids.T, got, router.T, gate_weight[0], up_weight[0], down_weight[0],
        specs=[VMEM] * 6,
        scratch=[
            pltpu.VMEM((n_e * n_b, n_e), F32)],
    )
    got = swap(sent.reshape(n_r * n_e, rows, size), ("rows", "expert"))
    width = n_h * size // n_c
    sent = call(
        functools.partial(split_kernel, width), struct((n_c, n_b, 128), F32),
        got, share, hidden, specs=[VMEM, VMEM, VMEM],
    )
    return call(sum_kernel, struct((n_b, width), BF16), swap(sent, "ctx"), specs=[VMEM])


def solution(mesh):
    placed = (
        P("expert", "rows", None),
        P("expert", "rows", "ctx", None),
        P("expert", "rows", "ctx", None),
        P("expert", "rows"),
        P("expert"),
        P("expert", None),
        P(),
        P("expert", None, ("rows", "ctx")),
        P("expert", None, ("rows", "ctx")),
        P("expert", ("rows", "ctx"), None),
    )
    return jax.shard_map(
        body, mesh=mesh, in_specs=placed, out_specs=P("expert", ("rows", "ctx")), check_vma=False
    )
```

```python
import functools
import math

import jax
import jax.numpy as jnp
from jax import lax
from jax.experimental import pallas as pl
from jax.experimental.pallas import tpu as pltpu
from jax.sharding import PartitionSpec as P

ITERS = 12
VMEM = pl.BlockSpec(memory_space=pltpu.VMEM)
SMEM = pl.BlockSpec(memory_space=pltpu.SMEM)
F32 = jnp.float32
BF16 = jnp.bfloat16
NEG = -1e30
FAR = 1.25
SCALE = 143.0
SHIFT = 80.0
HBM = pl.BlockSpec(memory_space=pltpu.HBM)
NT = (((1,), (1,)), ((), ()))


def call(kernel, outs, *args, specs, out_spec=VMEM, scratch=(), limit=16 << 20):
    return pl.pallas_call(
        kernel,
        out_shape=outs,
        in_specs=specs,
        out_specs=jax.tree.map(lambda _: out_spec, outs),
        scratch_shapes=scratch,
        compiler_params=pltpu.CompilerParams(vmem_limit_bytes=limit),
        cost_estimate=pl.CostEstimate(flops=1 << 36, bytes_accessed=1 << 28, transcendentals=0),
    )(*args)


def iota(shape, dim):
    return lax.broadcasted_iota(jnp.int32, shape, dim)


def one_hot(mask):
    return jnp.where(mask, 1.0, 0.0).astype(BF16)


def parts_of(x, count):
    parts = []
    for _ in range(count):
        part = x.astype(BF16)
        parts.append(part)
        x = x - part.astype(F32)
    return parts


def score_kernel(
    heads, k_hbm, q_hbm, len_hbm, v_hbm, out_hbm, out_ref, k_ref, q_ref, len_ref, v_ref, sems, out_sems
):
    pairs = ((k_hbm, k_ref), (q_hbm, q_ref), (len_hbm, len_ref), (v_hbm, v_ref))
    copies = [pltpu.make_async_copy(src, dst, sems.at[i]) for i, (src, dst) in enumerate(pairs)]
    for copy in copies:
        copy.start()
    n_b, here, size = k_ref.shape
    split = out_ref.shape[0] // n_b
    dims = size // split
    c = lax.axis_index("ctx")
    place = c * here + iota((8, here), 1)
    eye = one_hot(iota((size, size), 0) == iota((size, size), 1))
    diagonal = iota((8, here), 0) == iota((8, here), 1)
    at, src = iota((8 * n_b, heads * n_b), 0), iota((8 * n_b, heads * n_b), 1)
    pick = one_hot(src == at % 8 * n_b + at // 8)
    for copy in copies[:3]:
        copy.wait()
    q = jnp.dot(pick, q_ref[...], preferred_element_type=F32)
    tails = []
    for b in range(n_b):
        q_b = q[8 * b:8 * b + 8].astype(BF16)
        scaled = lax.dot_general(q_b, k_ref[b], NT, preferred_element_type=F32) * (0.5 / math.sqrt(size))
        valid = place < len_ref[b]
        top = jnp.max(jnp.where(valid, scaled, NEG), axis=-1, keepdims=True)
        coarse = top.astype(BF16).astype(F32)
        fine = top - coarse
        fine = (fine + jnp.abs(fine) * (1.0 / 128.0)).astype(BF16).astype(F32)
        below = jnp.where(valid, jnp.minimum((coarse + fine) - scaled, FAR), FAR)
        coded = jnp.exp(SCALE * jnp.sqrt(jnp.maximum(below, 0.0)) - SHIFT)
        count = jnp.sum(jnp.where(valid, 1.0, 0.0)[0:1], axis=-1, keepdims=True)
        tops = [jnp.sum(jnp.where(diagonal, part, 0.0), axis=0, keepdims=True) for part in (coarse, fine)]
        lane = iota((1, here), 1)
        tops[0] = jnp.where(lane < 8, tops[0], count)
        rows = [coded[0:heads]] + tops
        tails.append(jnp.concatenate(rows, axis=0))
    copies[3].wait()
    out_copies = []
    for b in range(n_b):
        turned = lax.dot_general(eye, v_ref[b], NT, preferred_element_type=F32)
        for j in range(split):
            block = jnp.concatenate([turned[j * dims:(j + 1) * dims], tails[b]], axis=0)
            out_ref[b * split + j] = block.astype(BF16)
        cut = pl.ds(b * split, split)
        out_copies.append(pltpu.make_async_copy(out_ref.at[cut], out_hbm.at[cut], out_sems.at[b]))
        out_copies[b].start()
    for copy in out_copies:
        copy.wait()


def attend_kernel(heads, split, got_ref, res_ref, out_ref):
    n_c, rows, here = got_ref.shape
    dims = rows - 8
    b, j = lax.axis_index("ctx") // split, lax.axis_index("ctx") % split
    parts = got_ref[:, dims:].astype(F32)
    diagonal = iota((n_c, 8, here), 1) == iota((n_c, 8, here), 2)
    tops = parts[:, heads:heads + 1] + parts[:, heads + 1:heads + 2]
    tops = jnp.sum(jnp.where(diagonal, tops, 0.0), axis=-1, keepdims=True)
    root = (jnp.log(parts) + SHIFT) * (1.0 / SCALE)
    scores = jnp.where(iota(root.shape, 1) < heads, tops - root * root, NEG)
    count = jnp.sum(parts[:, heads:heads + 1, 8:9], axis=0)
    top = jnp.max(jnp.max(scores, axis=0), axis=-1, keepdims=True)
    low = top - 1.0
    interval = (top - 1.0 / jnp.sqrt(count)) - low

    def mass(middle):
        excess = jnp.maximum(scores - middle[None], 0.0)
        return jnp.sum(jnp.sum(excess * excess, axis=0), axis=-1, keepdims=True)

    for _ in range(ITERS // 3):
        w1 = interval / 2.0
        w2 = w1 / 2.0
        w3 = w2 / 2.0
        m1 = low + w1
        m2 = (low + w2, m1 + w2)
        m3 = (low + w3, m2[0] + w3, m1 + w3, m2[1] + w3)
        t1, t2, t3 = mass(m1), [mass(m) for m in m2], [mass(m) for m in m3]
        c1 = t1 >= 1.0
        low = jnp.where(c1, m1, low)
        c2 = jnp.where(c1, t2[1], t2[0]) >= 1.0
        low = jnp.where(c2, jnp.where(c1, m2[1], m2[0]), low)
        middle = jnp.where(c1, jnp.where(c2, m3[3], m3[2]), jnp.where(c2, m3[1], m3[0]))
        total = jnp.where(c1, jnp.where(c2, t3[3], t3[2]), jnp.where(c2, t3[1], t3[0]))
        low = jnp.where(total >= 1.0, middle, low)
        interval = w3
    excess = jnp.maximum(scores - middle[None], 0.0)
    weights = excess * excess
    weights = jnp.concatenate([weights[i] for i in range(n_c)], axis=1).astype(BF16)
    values = jnp.concatenate([got_ref[i, 0:dims] for i in range(n_c)], axis=1)
    attended = lax.dot_general(weights, values, NT, preferred_element_type=F32) / total
    res = res_ref[...].astype(F32)
    res = jnp.sum(jnp.where(iota(res.shape, 0) == b, res, 0.0), axis=0, keepdims=True)
    res = [res[:, h * here:(h + 1) * here] for h in range(heads)]
    res = jnp.concatenate(res + [jnp.zeros((8 - heads, here), F32)], axis=0)
    mine = res[:, 0:dims]
    for k in range(1, split):
        mine = jnp.where(j == k, res[:, k * dims:(k + 1) * dims], mine)
    hidden = mine + attended
    flat = [hidden[h:h + 1] for h in range(heads)]
    flat += [jnp.zeros((1, dims), F32)] * (-heads % split)
    lines = [jnp.concatenate(flat[h:h + split], axis=1) for h in range(0, len(flat), split)]
    piece = jnp.concatenate(lines, axis=0).astype(BF16)
    for i in range(n_c):
        out_ref[i] = piece


def hidden_kernel(got_ref, hid_ref, out_ref):
    n_c = got_ref.shape[0]
    rows, size = hid_ref.shape
    n_b = 4
    split = n_c // n_b
    dims = size // split
    at, src = iota((n_c, n_c), 0), iota((n_c, n_c), 1)
    pick = one_hot(src == (at % n_b) * split + at // n_b)
    got = got_ref[...].astype(F32)
    moved = [
        jnp.dot(pick, got[:, k].astype(BF16), preferred_element_type=F32) for k in range(got_ref.shape[1])
    ]
    pieces = []
    for h in range(rows // n_b):
        lanes = slice(h % split * dims, (h % split + 1) * dims)
        from_j = [moved[h // split][j * n_b:(j + 1) * n_b, lanes] for j in range(split)]
        pieces.append(jnp.concatenate(from_j, axis=1))
    hidden = jnp.concatenate(pieces, axis=0).astype(BF16)
    hid_ref[...] = hidden
    for i in range(out_ref.shape[0]):
        out_ref[i] = hidden


def expert_kernel(
    ids_ref, g_ref, router_ref, gate_ref, up_ref, down_ref, out_ref, share_ref, logit_ref
):
    n_r, n_e, block, _ = out_ref.shape
    n_b = 4
    rows = n_e * n_b
    heads = block // n_b
    width = heads * 128
    at, src = iota((heads * rows, n_e * block), 0), iota((heads * rows, n_e * block), 1)
    inner = at % rows
    pick = one_hot(src == (inner // n_b) * block + (at // rows) * n_b + inner % n_b)
    at, src = iota((n_e * block, heads * rows), 0), iota((n_e * block, heads * rows), 1)
    inner = at % block
    back = one_hot(src == inner // n_b * rows + at // block * n_b + inner % n_b)
    router = jnp.concatenate([part.astype(F32) for part in parts_of(router_ref[...], 3)], axis=0).astype(BF16)
    gate = up = logits = None
    for r in range(n_r):
        moved = jnp.dot(pick, g_ref[r], preferred_element_type=F32).astype(BF16)
        x = jnp.concatenate([moved[h * rows:(h + 1) * rows] for h in range(heads)], axis=1)
        cols = slice(r * width, (r + 1) * width)
        g = jnp.dot(x, gate_ref[cols], preferred_element_type=F32)
        u = jnp.dot(x, up_ref[cols], preferred_element_type=F32)
        l = lax.dot_general(x, router[:, cols], NT, preferred_element_type=F32)
        gate, up, logits = (g, u, l) if r == 0 else (gate + g, up + u, logits + l)
    act = ((gate / (1.0 + jnp.exp(-gate))) * up).astype(BF16)
    for r in range(n_r):
        o = jnp.dot(act, down_ref[:, r * width:(r + 1) * width], preferred_element_type=F32).astype(BF16)
        o = jnp.concatenate([o[:, h * 128:(h + 1) * 128] for h in range(heads)], axis=0)
        o = jnp.dot(back, o, preferred_element_type=F32)
        for e in range(n_e):
            out_ref[r, e] = o[e * block:(e + 1) * block].astype(BF16)
    logit_ref[...] = (logits[:, 2 * n_e:3 * n_e] + logits[:, n_e:2 * n_e]) + logits[:, 0:n_e]
    logits = logit_ref[pl.ds(lax.axis_index("expert") * n_b, n_b), :]
    logits = jnp.concatenate([logits] * heads, axis=0)
    which = iota(logits.shape, 1)
    owner = iota(logits.shape, 0) % n_b
    first = second = jnp.zeros(logits.shape, jnp.int32)
    for b in range(n_b):
        first = jnp.where(owner == b, ids_ref[0:1, b:b + 1], first)
        second = jnp.where(owner == b, ids_ref[1:2, b:b + 1], second)
    l0 = jnp.sum(jnp.where(which == first, logits, 0.0), axis=-1, keepdims=True)
    l1 = jnp.sum(jnp.where(which == second, logits, 0.0), axis=-1, keepdims=True)
    s0 = 1.0 / (1.0 + jnp.exp(l1 - l0))
    s1 = 1.0 / (1.0 + jnp.exp(l0 - l1))
    share_ref[...] = jnp.where(which == first, s0, 0.0) + jnp.where(which == second, s1, 0.0)


def split_kernel(width, parts_ref, share_ref, hid_ref, out_ref):
    n_c, n_b = out_ref.shape[0], 4
    n_e = share_ref.shape[1]
    n_r = parts_ref.shape[0] // n_e
    total = None
    for e in range(n_e):
        part = parts_ref[e].astype(F32)
        for r in range(1, n_r):
            part = part + parts_ref[r * n_e + e].astype(F32)
        part = part * share_ref[:, e:e + 1]
        total = part if total is None else total + part
    c = lax.axis_index("ctx")
    col = (iota(total.shape, 0) // n_b) * 128 + iota(total.shape, 1)
    mine = (col >= c * width) & (col < (c + 1) * width)
    total = total + jnp.where(mine, hid_ref[...].astype(F32), 0.0)
    for i in range(n_c):
        h, off = divmod(i * width, 128)
        n = min(width, 128 - off)
        piece = total[h * n_b:(h + 1) * n_b, off:off + n]
        if n < width:
            piece = jnp.concatenate([piece, total[(h + 1) * n_b:(h + 2) * n_b, 0:width - n]], axis=1)
        for b in range(n_b):
            out_ref[i, b // 2:b // 2 + 1, b % 2 * width:(b % 2 + 1) * width] = piece[b:b + 1]


def sum_kernel(parts_ref, out_ref):
    total = jnp.sum(parts_ref[...], axis=0)
    n_b, width = out_ref.shape
    rows = [total[b // 2:b // 2 + 1, b % 2 * width:(b % 2 + 1) * width] for b in range(n_b)]
    out_ref[...] = jnp.concatenate(rows, axis=0).astype(BF16)


def body(
    queries,
    cache_keys,
    cache_values,
    residual,
    lengths,
    expert_ids,
    router,
    gate_weight,
    up_weight,
    down_weight,
):
    n_b, n_h, size = queries.shape
    here = cache_keys.shape[2]
    n_c, n_r, n_e = (lax.axis_size(a) for a in ("ctx", "rows", "expert"))
    rows = n_b * n_h
    struct = jax.ShapeDtypeStruct
    q = queries.transpose(1, 0, 2).reshape(rows, size)
    keys = cache_keys.reshape(n_b, here, size)
    values = cache_values.reshape(n_b, here, size)

    def swap(x, axes):
        return lax.all_to_all(x, axes, split_axis=0, concat_axis=0, tiled=True)

    dims = size * n_b // n_c
    sent = call(
        functools.partial(score_kernel, n_h), struct((n_c, dims + 8, here), BF16),
        keys, q, lengths, values, specs=[HBM] * 4, out_spec=HBM,
        scratch=[
            pltpu.VMEM((n_c, dims + 8, here), BF16), pltpu.VMEM(keys.shape, BF16), pltpu.VMEM(q.shape, BF16),
            pltpu.SMEM((n_b,), jnp.int32), pltpu.VMEM(values.shape, BF16),
            pltpu.SemaphoreType.DMA((4,)), pltpu.SemaphoreType.DMA((n_b,)),
        ],
        limit=60 << 20,
    )
    got = swap(sent, "ctx")
    sent = call(
        functools.partial(attend_kernel, n_h, n_c // n_b), struct((n_c, -(-n_h * n_b // n_c), size), BF16), got, residual,
        specs=[VMEM, VMEM],
    )
    got = swap(sent, "ctx")
    hidden, sent = call(
        hidden_kernel, (struct((rows, size), BF16), struct((n_r * n_e, rows, size), BF16)), got, specs=[VMEM],
    )
    got = swap(sent, ("rows", "expert")).reshape(n_r, n_e * rows, size)
    sent, share = call(
        expert_kernel, (struct((n_r, n_e, rows, size), BF16), struct((rows, n_e), F32)),
        expert_ids.T, got, router.T, gate_weight[0], up_weight[0], down_weight[0],
        specs=[VMEM] * 6,
        scratch=[
            pltpu.VMEM((n_e * n_b, n_e), F32)],
    )
    got = swap(sent.reshape(n_r * n_e, rows, size), ("rows", "expert"))
    width = n_h * size // n_c
    sent = call(
        functools.partial(split_kernel, width), struct((n_c, n_b // 2, 2 * width), F32),
        got, share, hidden, specs=[VMEM, VMEM, VMEM],
    )
    return call(sum_kernel, struct((n_b, width), BF16), swap(sent, "ctx"), specs=[VMEM])


def solution(mesh):
    placed = (
        P("expert", "rows", None),
        P("expert", "rows", "ctx", None),
        P("expert", "rows", "ctx", None),
        P("expert", "rows"),
        P("expert"),
        P("expert", None),
        P(),
        P("expert", None, ("rows", "ctx")),
        P("expert", None, ("rows", "ctx")),
        P("expert", ("rows", "ctx"), None),
    )
    return jax.shard_map(
        body, mesh=mesh, in_specs=placed, out_specs=P("expert", ("rows", "ctx")), check_vma=False
    )
```

```python
import functools
import math

import jax
import jax.numpy as jnp
from jax import lax
from jax.experimental import pallas as pl
from jax.experimental.pallas import tpu as pltpu
from jax.sharding import PartitionSpec as P

ITERS = 12
VMEM = pl.BlockSpec(memory_space=pltpu.VMEM)
SMEM = pl.BlockSpec(memory_space=pltpu.SMEM)
F32 = jnp.float32
BF16 = jnp.bfloat16
NEG = -1e30
FAR = 1.25
SCALE = 206.0
SHIFT = 115.0
HBM = pl.BlockSpec(memory_space=pltpu.HBM)
NT = (((1,), (1,)), ((), ()))


def call(kernel, outs, *args, specs, out_spec=VMEM, scratch=(), limit=16 << 20):
    return pl.pallas_call(
        kernel,
        out_shape=outs,
        in_specs=specs,
        out_specs=jax.tree.map(lambda _: out_spec, outs),
        scratch_shapes=scratch,
        compiler_params=pltpu.CompilerParams(vmem_limit_bytes=limit),
        cost_estimate=pl.CostEstimate(flops=1 << 36, bytes_accessed=1 << 28, transcendentals=0),
    )(*args)


def iota(shape, dim):
    return lax.broadcasted_iota(jnp.int32, shape, dim)


def one_hot(mask):
    return jnp.where(mask, 1.0, 0.0).astype(BF16)


def parts_of(x, count):
    parts = []
    for _ in range(count):
        part = x.astype(BF16)
        parts.append(part)
        x = x - part.astype(F32)
    return parts


def score_kernel(
    heads, k_hbm, q_hbm, len_hbm, v_hbm, out_hbm, out_ref, k_ref, q_ref, len_ref, v_ref, sems, out_sems
):
    pairs = ((k_hbm, k_ref), (q_hbm, q_ref), (len_hbm, len_ref), (v_hbm, v_ref))
    copies = [pltpu.make_async_copy(src, dst, sems.at[i]) for i, (src, dst) in enumerate(pairs)]
    for copy in copies:
        copy.start()
    n_b, here, size = k_ref.shape
    split = out_ref.shape[0] // n_b
    dims = size // split
    c = lax.axis_index("ctx")
    place = c * here + iota((8, here), 1)
    eye = one_hot(iota((size, size), 0) == iota((size, size), 1))
    diagonal = iota((8, here), 0) == iota((8, here), 1)
    at, src = iota((8 * n_b, heads * n_b), 0), iota((8 * n_b, heads * n_b), 1)
    pick = one_hot(src == at % 8 * n_b + at // 8)
    for copy in copies[:3]:
        copy.wait()
    q = jnp.dot(pick, q_ref[...], preferred_element_type=F32)
    tails = []
    for b in range(n_b):
        q_b = q[8 * b:8 * b + 8].astype(BF16)
        scaled = lax.dot_general(q_b, k_ref[b], NT, preferred_element_type=F32) * (0.5 / math.sqrt(size))
        valid = place < len_ref[b]
        top = jnp.max(jnp.where(valid, scaled, NEG), axis=-1, keepdims=True)
        coarse = top.astype(BF16).astype(F32)
        fine = top - coarse
        fine = (fine + jnp.abs(fine) * (1.0 / 128.0)).astype(BF16).astype(F32)
        below = jnp.where(valid, jnp.minimum((coarse + fine) - scaled, FAR), FAR)
        coded = jnp.exp2(SCALE * jnp.sqrt(jnp.maximum(below, 0.0)) - SHIFT)
        count = jnp.minimum(jnp.maximum(len_ref[b] - c * here, 0), here).astype(F32)
        tops = [jnp.sum(jnp.where(diagonal, part, 0.0), axis=0, keepdims=True) for part in (coarse, fine)]
        lane = iota((1, here), 1)
        tops[0] = jnp.where(lane < 8, tops[0], count)
        rows = [coded[0:heads]] + tops
        tails.append(jnp.concatenate(rows, axis=0))
    copies[3].wait()
    out_copies = []
    for b in range(n_b):
        turned = lax.dot_general(eye, v_ref[b], NT, preferred_element_type=F32)
        for j in range(split):
            block = jnp.concatenate([turned[j * dims:(j + 1) * dims], tails[b]], axis=0)
            out_ref[b * split + j] = block.astype(BF16)
        cut = pl.ds(b * split, split)
        out_copies.append(pltpu.make_async_copy(out_ref.at[cut], out_hbm.at[cut], out_sems.at[b]))
        out_copies[b].start()
    for copy in out_copies:
        copy.wait()


def attend_kernel(heads, split, got_ref, res_ref, out_ref):
    n_c, rows, here = got_ref.shape
    dims = rows - 8
    b, j = lax.axis_index("ctx") // split, lax.axis_index("ctx") % split
    row = jnp.dot(one_hot(iota((8, res_ref.shape[0]), 1) == b), res_ref[...], preferred_element_type=F32)
    res = row[:, 0:here]
    for h in range(1, heads):
        res = jnp.where(iota(res.shape, 0) == h, row[:, h * here:(h + 1) * here], res)
    mine = res[:, 0:dims]
    for k in range(1, split):
        mine = jnp.where(j == k, res[:, k * dims:(k + 1) * dims], mine)
    parts = got_ref[:, dims:].astype(F32)
    diagonal = iota((n_c, 8, here), 1) == iota((n_c, 8, here), 2)
    tops = parts[:, heads:heads + 1] + parts[:, heads + 1:heads + 2]
    tops = jnp.sum(jnp.where(diagonal, tops, 0.0), axis=-1, keepdims=True)
    root = (jnp.log2(parts) + SHIFT) * (1.0 / SCALE)
    scores = jnp.where(iota(root.shape, 1) < heads, tops - root * root, NEG)
    count = jnp.sum(parts[:, heads:heads + 1, 8:9], axis=0)
    top = jnp.max(jnp.max(scores, axis=0), axis=-1, keepdims=True)
    low = top - 1.0
    interval = (top - 1.0 / jnp.sqrt(count)) - low

    def mass(middle):
        excess = jnp.maximum(scores - middle[None], 0.0)
        return jnp.sum(jnp.sum(excess * excess, axis=0), axis=-1, keepdims=True)

    for _ in range(ITERS // 3):
        w1 = interval / 2.0
        w2 = w1 / 2.0
        w3 = w2 / 2.0
        m1 = low + w1
        m2 = (low + w2, m1 + w2)
        m3 = (low + w3, m2[0] + w3, m1 + w3, m2[1] + w3)
        t1, t2, t3 = mass(m1), [mass(m) for m in m2], [mass(m) for m in m3]
        c1 = t1 >= 1.0
        low = jnp.where(c1, m1, low)
        c2 = jnp.where(c1, t2[1], t2[0]) >= 1.0
        low = jnp.where(c2, jnp.where(c1, m2[1], m2[0]), low)
        middle = jnp.where(c1, jnp.where(c2, m3[3], m3[2]), jnp.where(c2, m3[1], m3[0]))
        total = jnp.where(c1, jnp.where(c2, t3[3], t3[2]), jnp.where(c2, t3[1], t3[0]))
        low = jnp.where(total >= 1.0, middle, low)
        interval = w3
    excess = jnp.maximum(scores - middle[None], 0.0)
    weights = excess * excess
    weights = jnp.concatenate([weights[i] for i in range(n_c)], axis=1).astype(BF16)
    values = jnp.concatenate([got_ref[i, 0:dims] for i in range(n_c)], axis=1)
    attended = lax.dot_general(weights, values, NT, preferred_element_type=F32) / total
    hidden = mine + attended
    flat = [hidden[h:h + 1] for h in range(heads)]
    flat += [jnp.zeros((1, dims), F32)] * (-heads % split)
    lines = [jnp.concatenate(flat[h:h + split], axis=1) for h in range(0, len(flat), split)]
    piece = jnp.concatenate(lines, axis=0).astype(BF16)
    for i in range(n_c):
        out_ref[i] = piece


def hidden_kernel(got_ref, hid_ref, out_ref):
    n_c = got_ref.shape[0]
    rows, size = hid_ref.shape
    n_b = 4
    split = n_c // n_b
    dims = size // split
    at, src = iota((n_c, n_c), 0), iota((n_c, n_c), 1)
    pick = one_hot(src == (at % n_b) * split + at // n_b)
    got = got_ref[...].astype(F32)
    moved = [
        jnp.dot(pick, got[:, k].astype(BF16), preferred_element_type=F32) for k in range(got_ref.shape[1])
    ]
    pieces = []
    for h in range(rows // n_b):
        lanes = slice(h % split * dims, (h % split + 1) * dims)
        from_j = [moved[h // split][j * n_b:(j + 1) * n_b, lanes] for j in range(split)]
        pieces.append(jnp.concatenate(from_j, axis=1))
    hidden = jnp.concatenate(pieces, axis=0).astype(BF16)
    hid_ref[...] = hidden
    for i in range(out_ref.shape[0]):
        out_ref[i] = hidden


def expert_kernel(
    ids_ref, g_ref, router_ref, gate_ref, up_ref, down_ref, out_ref, share_ref, logit_ref
):
    n_r, n_e, block, _ = out_ref.shape
    n_b = 4
    rows = n_e * n_b
    heads = block // n_b
    width = heads * 128
    at, src = iota((heads * rows, n_e * block), 0), iota((heads * rows, n_e * block), 1)
    inner = at % rows
    pick = one_hot(src == (inner // n_b) * block + (at // rows) * n_b + inner % n_b)
    at, src = iota((n_e * block, heads * rows), 0), iota((n_e * block, heads * rows), 1)
    inner = at % block
    back = one_hot(src == inner // n_b * rows + at // block * n_b + inner % n_b)
    router = jnp.concatenate([part.astype(F32) for part in parts_of(router_ref[...], 3)], axis=0).astype(BF16)
    gate = up = logits = None
    for r in range(n_r):
        moved = jnp.dot(pick, g_ref[r], preferred_element_type=F32).astype(BF16)
        x = jnp.concatenate([moved[h * rows:(h + 1) * rows] for h in range(heads)], axis=1)
        cols = slice(r * width, (r + 1) * width)
        g = jnp.dot(x, gate_ref[cols], preferred_element_type=F32)
        u = jnp.dot(x, up_ref[cols], preferred_element_type=F32)
        l = lax.dot_general(x, router[:, cols], NT, preferred_element_type=F32)
        gate, up, logits = (g, u, l) if r == 0 else (gate + g, up + u, logits + l)
    act = ((gate / (1.0 + jnp.exp(-gate))) * up).astype(BF16)
    for r in range(n_r):
        o = jnp.dot(act, down_ref[:, r * width:(r + 1) * width], preferred_element_type=F32).astype(BF16)
        o = jnp.concatenate([o[:, h * 128:(h + 1) * 128] for h in range(heads)], axis=0)
        o = jnp.dot(back, o, preferred_element_type=F32)
        for e in range(n_e):
            out_ref[r, e] = o[e * block:(e + 1) * block].astype(BF16)
    logit_ref[...] = (logits[:, 2 * n_e:3 * n_e] + logits[:, n_e:2 * n_e]) + logits[:, 0:n_e]
    logits = logit_ref[pl.ds(lax.axis_index("expert") * n_b, n_b), :]
    logits = jnp.concatenate([logits] * heads, axis=0)
    which = iota(logits.shape, 1)
    owner = iota(logits.shape, 0) % n_b
    first = second = jnp.zeros(logits.shape, jnp.int32)
    for b in range(n_b):
        first = jnp.where(owner == b, ids_ref[0:1, b:b + 1], first)
        second = jnp.where(owner == b, ids_ref[1:2, b:b + 1], second)
    l0 = jnp.sum(jnp.where(which == first, logits, 0.0), axis=-1, keepdims=True)
    l1 = jnp.sum(jnp.where(which == second, logits, 0.0), axis=-1, keepdims=True)
    s0 = 1.0 / (1.0 + jnp.exp(l1 - l0))
    s1 = 1.0 / (1.0 + jnp.exp(l0 - l1))
    share_ref[...] = jnp.where(which == first, s0, 0.0) + jnp.where(which == second, s1, 0.0)


def split_kernel(width, parts_ref, share_ref, hid_ref, out_ref):
    n_c, n_b = out_ref.shape[0], 4
    n_e = share_ref.shape[1]
    n_r = parts_ref.shape[0] // n_e
    total = None
    for e in range(n_e):
        part = parts_ref[e].astype(F32)
        for r in range(1, n_r):
            part = part + parts_ref[r * n_e + e].astype(F32)
        part = part * share_ref[:, e:e + 1]
        total = part if total is None else total + part
    c = lax.axis_index("ctx")
    col = (iota(total.shape, 0) // n_b) * 128 + iota(total.shape, 1)
    mine = (col >= c * width) & (col < (c + 1) * width)
    total = total + jnp.where(mine, hid_ref[...].astype(F32), 0.0)
    for i in range(n_c):
        h, off = divmod(i * width, 128)
        n = min(width, 128 - off)
        piece = total[h * n_b:(h + 1) * n_b, off:off + n]
        if n < width:
            piece = jnp.concatenate([piece, total[(h + 1) * n_b:(h + 2) * n_b, 0:width - n]], axis=1)
        for b in range(n_b):
            out_ref[i, b // 2:b // 2 + 1, b % 2 * width:(b % 2 + 1) * width] = piece[b:b + 1]


def sum_kernel(parts_ref, out_ref):
    total = jnp.sum(parts_ref[...], axis=0)
    n_b, width = out_ref.shape
    rows = [total[b // 2:b // 2 + 1, b % 2 * width:(b % 2 + 1) * width] for b in range(n_b)]
    out_ref[...] = jnp.concatenate(rows, axis=0).astype(BF16)


def body(
    queries,
    cache_keys,
    cache_values,
    residual,
    lengths,
    expert_ids,
    router,
    gate_weight,
    up_weight,
    down_weight,
):
    n_b, n_h, size = queries.shape
    here = cache_keys.shape[2]
    n_c, n_r, n_e = (lax.axis_size(a) for a in ("ctx", "rows", "expert"))
    rows = n_b * n_h
    struct = jax.ShapeDtypeStruct
    q = queries.transpose(1, 0, 2).reshape(rows, size)
    keys = cache_keys.reshape(n_b, here, size)
    values = cache_values.reshape(n_b, here, size)

    def swap(x, axes):
        return lax.all_to_all(x, axes, split_axis=0, concat_axis=0, tiled=True)

    dims = size * n_b // n_c
    sent = call(
        functools.partial(score_kernel, n_h), struct((n_c, dims + 8, here), BF16),
        keys, q, lengths, values, specs=[HBM] * 4, out_spec=HBM,
        scratch=[
            pltpu.VMEM((n_c, dims + 8, here), BF16), pltpu.VMEM(keys.shape, BF16), pltpu.VMEM(q.shape, BF16),
            pltpu.SMEM((n_b,), jnp.int32), pltpu.VMEM(values.shape, BF16),
            pltpu.SemaphoreType.DMA((4,)), pltpu.SemaphoreType.DMA((n_b,)),
        ],
        limit=60 << 20,
    )
    got = swap(sent, "ctx")
    sent = call(
        functools.partial(attend_kernel, n_h, n_c // n_b), struct((n_c, -(-n_h * n_b // n_c), size), BF16), got, residual,
        specs=[VMEM, VMEM],
    )
    got = swap(sent, "ctx")
    hidden, sent = call(
        hidden_kernel, (struct((rows, size), BF16), struct((n_r * n_e, rows, size), BF16)), got, specs=[VMEM],
    )
    got = swap(sent, ("rows", "expert")).reshape(n_r, n_e * rows, size)
    sent, share = call(
        expert_kernel, (struct((n_r, n_e, rows, size), BF16), struct((rows, n_e), F32)),
        expert_ids.T, got, router.T, gate_weight[0], up_weight[0], down_weight[0],
        specs=[VMEM] * 6,
        scratch=[
            pltpu.VMEM((n_e * n_b, n_e), F32)],
    )
    got = swap(sent.reshape(n_r * n_e, rows, size), ("rows", "expert"))
    width = n_h * size // n_c
    sent = call(
        functools.partial(split_kernel, width), struct((n_c, n_b // 2, 2 * width), F32),
        got, share, hidden, specs=[VMEM, VMEM, VMEM],
    )
    return call(sum_kernel, struct((n_b, width), BF16), swap(sent, "ctx"), specs=[VMEM])


def solution(mesh):
    placed = (
        P("expert", "rows", None),
        P("expert", "rows", "ctx", None),
        P("expert", "rows", "ctx", None),
        P("expert", "rows"),
        P("expert"),
        P("expert", None),
        P(),
        P("expert", None, ("rows", "ctx")),
        P("expert", None, ("rows", "ctx")),
        P("expert", ("rows", "ctx"), None),
    )
    return jax.shard_map(
        body, mesh=mesh, in_specs=placed, out_specs=P("expert", ("rows", "ctx")), check_vma=False
    )
```

```python
import functools
import math

import jax
import jax.numpy as jnp
from jax import lax
from jax.experimental import pallas as pl
from jax.experimental.pallas import tpu as pltpu
from jax.sharding import PartitionSpec as P

ITERS = 12
VMEM = pl.BlockSpec(memory_space=pltpu.VMEM)
SMEM = pl.BlockSpec(memory_space=pltpu.SMEM)
F32 = jnp.float32
BF16 = jnp.bfloat16
NEG = -1e30
FAR = 1.25
SCALE = 206.0
SHIFT = 115.0
HBM = pl.BlockSpec(memory_space=pltpu.HBM)
NT = (((1,), (1,)), ((), ()))


def call(kernel, outs, *args, specs, out_spec=VMEM, scratch=(), limit=16 << 20):
    return pl.pallas_call(
        kernel,
        out_shape=outs,
        in_specs=specs,
        out_specs=jax.tree.map(lambda _: out_spec, outs),
        scratch_shapes=scratch,
        compiler_params=pltpu.CompilerParams(vmem_limit_bytes=limit),
        cost_estimate=pl.CostEstimate(flops=1 << 36, bytes_accessed=1 << 28, transcendentals=0),
    )(*args)


def iota(shape, dim):
    return lax.broadcasted_iota(jnp.int32, shape, dim)


def one_hot(mask):
    return jnp.where(mask, 1.0, 0.0).astype(BF16)


def parts_of(x, count):
    parts = []
    for _ in range(count):
        part = x.astype(BF16)
        parts.append(part)
        x = x - part.astype(F32)
    return parts


def score_kernel(
    heads, k_hbm, q_hbm, len_hbm, v_hbm, out_hbm, out_ref, k_ref, q_ref, len_ref, v_ref, sems, out_sems
):
    pairs = ((k_hbm, k_ref), (q_hbm, q_ref), (len_hbm, len_ref), (v_hbm, v_ref))
    copies = [pltpu.make_async_copy(src, dst, sems.at[i]) for i, (src, dst) in enumerate(pairs)]
    for copy in copies:
        copy.start()
    n_b, here, size = k_ref.shape
    split = out_ref.shape[0] // n_b
    dims = size // split
    c = lax.axis_index("ctx")
    place = c * here + iota((8, here), 1)
    eye = one_hot(iota((size, size), 0) == iota((size, size), 1))
    diagonal = iota((8, here), 0) == iota((8, here), 1)
    at, src = iota((8 * n_b, heads * n_b), 0), iota((8 * n_b, heads * n_b), 1)
    pick = one_hot(src == at % 8 * n_b + at // 8)
    for copy in copies:
        copy.wait()
    q = jnp.dot(pick, q_ref[...], preferred_element_type=F32)
    out_copies = []
    for b in range(n_b):
        q_b = q[8 * b:8 * b + 8].astype(BF16)
        scaled = lax.dot_general(q_b, k_ref[b], NT, preferred_element_type=F32) * (0.5 / math.sqrt(size))
        valid = place < len_ref[b]
        top = jnp.max(jnp.where(valid, scaled, NEG), axis=-1, keepdims=True)
        coarse = top.astype(BF16).astype(F32)
        fine = top - coarse
        fine = (fine + jnp.abs(fine) * (1.0 / 128.0)).astype(BF16).astype(F32)
        below = jnp.where(valid, jnp.minimum((coarse + fine) - scaled, FAR), FAR)
        coded = jnp.exp2(SCALE * jnp.sqrt(jnp.maximum(below, 0.0)) - SHIFT)
        count = jnp.minimum(jnp.maximum(len_ref[b] - c * here, 0), here).astype(F32)
        tops = [jnp.sum(jnp.where(diagonal, part, 0.0), axis=0, keepdims=True) for part in (coarse, fine)]
        lane = iota((1, here), 1)
        tops[0] = jnp.where(lane < 8, tops[0], count)
        rows = [coded[0:heads]] + tops
        tail = jnp.concatenate(rows, axis=0)
        turned = lax.dot_general(eye, v_ref[b], NT, preferred_element_type=F32)
        for j in range(split):
            block = jnp.concatenate([turned[j * dims:(j + 1) * dims], tail], axis=0)
            out_ref[b * split + j] = block.astype(BF16)
        cut = pl.ds(b * split, split)
        out_copies.append(pltpu.make_async_copy(out_ref.at[cut], out_hbm.at[cut], out_sems.at[b]))
        out_copies[b].start()
    for copy in out_copies:
        copy.wait()


def attend_kernel(heads, split, got_ref, res_ref, out_ref):
    n_c, rows, here = got_ref.shape
    dims = rows - 8
    b, j = lax.axis_index("ctx") // split, lax.axis_index("ctx") % split
    row = jnp.dot(one_hot(iota((8, res_ref.shape[0]), 1) == b), res_ref[...], preferred_element_type=F32)
    res = row[:, 0:here]
    for h in range(1, heads):
        res = jnp.where(iota(res.shape, 0) == h, row[:, h * here:(h + 1) * here], res)
    mine = res[:, 0:dims]
    for k in range(1, split):
        mine = jnp.where(j == k, res[:, k * dims:(k + 1) * dims], mine)
    parts = got_ref[:, dims:].astype(F32)
    diagonal = iota((n_c, 8, here), 1) == iota((n_c, 8, here), 2)
    tops = parts[:, heads:heads + 1] + parts[:, heads + 1:heads + 2]
    tops = jnp.sum(jnp.where(diagonal, tops, 0.0), axis=-1, keepdims=True)
    root = (jnp.log2(parts) + SHIFT) * (1.0 / SCALE)
    scores = jnp.where(iota(root.shape, 1) < heads, tops - root * root, NEG)
    count = jnp.sum(parts[:, heads:heads + 1, 8:9], axis=0)
    top = jnp.max(jnp.max(scores, axis=0), axis=-1, keepdims=True)
    low = top - 1.0
    interval = (top - 1.0 / jnp.sqrt(count)) - low

    def mass(middle):
        excess = jnp.maximum(scores - middle[None], 0.0)
        return jnp.sum(jnp.sum(excess * excess, axis=0), axis=-1, keepdims=True)

    for _ in range(ITERS // 3):
        w1 = interval / 2.0
        w2 = w1 / 2.0
        w3 = w2 / 2.0
        m1 = low + w1
        m2 = (low + w2, m1 + w2)
        m3 = (low + w3, m2[0] + w3, m1 + w3, m2[1] + w3)
        t1, t2, t3 = mass(m1), [mass(m) for m in m2], [mass(m) for m in m3]
        c1 = t1 >= 1.0
        low = jnp.where(c1, m1, low)
        c2 = jnp.where(c1, t2[1], t2[0]) >= 1.0
        low = jnp.where(c2, jnp.where(c1, m2[1], m2[0]), low)
        middle = jnp.where(c1, jnp.where(c2, m3[3], m3[2]), jnp.where(c2, m3[1], m3[0]))
        total = jnp.where(c1, jnp.where(c2, t3[3], t3[2]), jnp.where(c2, t3[1], t3[0]))
        low = jnp.where(total >= 1.0, middle, low)
        interval = w3
    excess = jnp.maximum(scores - middle[None], 0.0)
    weights = excess * excess
    weights = jnp.concatenate([weights[i] for i in range(n_c)], axis=1).astype(BF16)
    values = jnp.concatenate([got_ref[i, 0:dims] for i in range(n_c)], axis=1)
    attended = lax.dot_general(weights, values, NT, preferred_element_type=F32) / total
    hidden = mine + attended
    flat = [hidden[h:h + 1] for h in range(heads)]
    flat += [jnp.zeros((1, dims), F32)] * (-heads % split)
    lines = [jnp.concatenate(flat[h:h + split], axis=1) for h in range(0, len(flat), split)]
    piece = jnp.concatenate(lines, axis=0).astype(BF16)
    for i in range(n_c):
        out_ref[i] = piece


def hidden_kernel(got_ref, hid_ref, out_ref):
    n_c = got_ref.shape[0]
    rows, size = hid_ref.shape
    n_b = 4
    split = n_c // n_b
    dims = size // split
    at, src = iota((n_c, n_c), 0), iota((n_c, n_c), 1)
    pick = one_hot(src == (at % n_b) * split + at // n_b)
    got = got_ref[...].astype(F32)
    moved = [
        jnp.dot(pick, got[:, k].astype(BF16), preferred_element_type=F32) for k in range(got_ref.shape[1])
    ]
    pieces = []
    for h in range(rows // n_b):
        lanes = slice(h % split * dims, (h % split + 1) * dims)
        from_j = [moved[h // split][j * n_b:(j + 1) * n_b, lanes] for j in range(split)]
        pieces.append(jnp.concatenate(from_j, axis=1))
    hidden = jnp.concatenate(pieces, axis=0).astype(BF16)
    hid_ref[...] = hidden
    for i in range(out_ref.shape[0]):
        out_ref[i] = hidden


def expert_kernel(
    ids_ref, g_ref, router_ref, gate_ref, up_ref, down_ref, out_ref, share_ref, logit_ref
):
    n_r, n_e, block, _ = out_ref.shape
    n_b = 4
    rows = n_e * n_b
    heads = block // n_b
    width = heads * 128
    at, src = iota((heads * rows, n_e * block), 0), iota((heads * rows, n_e * block), 1)
    inner = at % rows
    pick = one_hot(src == (inner // n_b) * block + (at // rows) * n_b + inner % n_b)
    at, src = iota((n_e * block, heads * rows), 0), iota((n_e * block, heads * rows), 1)
    inner = at % block
    back = one_hot(src == inner // n_b * rows + at // block * n_b + inner % n_b)
    router = jnp.concatenate([part.astype(F32) for part in parts_of(router_ref[...], 3)], axis=0).astype(BF16)
    gate = up = logits = None
    for r in range(n_r):
        moved = jnp.dot(pick, g_ref[r], preferred_element_type=F32).astype(BF16)
        x = jnp.concatenate([moved[h * rows:(h + 1) * rows] for h in range(heads)], axis=1)
        cols = slice(r * width, (r + 1) * width)
        g = jnp.dot(x, gate_ref[cols], preferred_element_type=F32)
        u = jnp.dot(x, up_ref[cols], preferred_element_type=F32)
        l = lax.dot_general(x, router[:, cols], NT, preferred_element_type=F32)
        gate, up, logits = (g, u, l) if r == 0 else (gate + g, up + u, logits + l)
    act = ((gate / (1.0 + jnp.exp(-gate))) * up).astype(BF16)
    for r in range(n_r):
        o = jnp.dot(act, down_ref[:, r * width:(r + 1) * width], preferred_element_type=F32).astype(BF16)
        o = jnp.concatenate([o[:, h * 128:(h + 1) * 128] for h in range(heads)], axis=0)
        o = jnp.dot(back, o, preferred_element_type=F32)
        for e in range(n_e):
            out_ref[r, e] = o[e * block:(e + 1) * block].astype(BF16)
    logit_ref[...] = (logits[:, 2 * n_e:3 * n_e] + logits[:, n_e:2 * n_e]) + logits[:, 0:n_e]
    logits = logit_ref[pl.ds(lax.axis_index("expert") * n_b, n_b), :]
    logits = jnp.concatenate([logits] * heads, axis=0)
    which = iota(logits.shape, 1)
    owner = iota(logits.shape, 0) % n_b
    first = second = jnp.zeros(logits.shape, jnp.int32)
    for b in range(n_b):
        first = jnp.where(owner == b, ids_ref[0:1, b:b + 1], first)
        second = jnp.where(owner == b, ids_ref[1:2, b:b + 1], second)
    l0 = jnp.sum(jnp.where(which == first, logits, 0.0), axis=-1, keepdims=True)
    l1 = jnp.sum(jnp.where(which == second, logits, 0.0), axis=-1, keepdims=True)
    s0 = 1.0 / (1.0 + jnp.exp(l1 - l0))
    s1 = 1.0 / (1.0 + jnp.exp(l0 - l1))
    share_ref[...] = jnp.where(which == first, s0, 0.0) + jnp.where(which == second, s1, 0.0)


def split_kernel(width, parts_ref, share_ref, hid_ref, out_ref):
    n_c, n_b = out_ref.shape[0], 4
    n_e = share_ref.shape[1]
    n_r = parts_ref.shape[0] // n_e
    total = None
    for e in range(n_e):
        part = parts_ref[e].astype(F32)
        for r in range(1, n_r):
            part = part + parts_ref[r * n_e + e].astype(F32)
        part = part * share_ref[:, e:e + 1]
        total = part if total is None else total + part
    c = lax.axis_index("ctx")
    col = (iota(total.shape, 0) // n_b) * 128 + iota(total.shape, 1)
    mine = (col >= c * width) & (col < (c + 1) * width)
    total = total + jnp.where(mine, hid_ref[...].astype(F32), 0.0)
    for i in range(n_c):
        h, off = divmod(i * width, 128)
        n = min(width, 128 - off)
        piece = total[h * n_b:(h + 1) * n_b, off:off + n]
        if n < width:
            piece = jnp.concatenate([piece, total[(h + 1) * n_b:(h + 2) * n_b, 0:width - n]], axis=1)
        for b in range(n_b):
            out_ref[i, b // 2:b // 2 + 1, b % 2 * width:(b % 2 + 1) * width] = piece[b:b + 1]


def sum_kernel(parts_ref, out_ref):
    total = jnp.sum(parts_ref[...], axis=0)
    n_b, width = out_ref.shape
    rows = [total[b // 2:b // 2 + 1, b % 2 * width:(b % 2 + 1) * width] for b in range(n_b)]
    out_ref[...] = jnp.concatenate(rows, axis=0).astype(BF16)


def body(
    queries,
    cache_keys,
    cache_values,
    residual,
    lengths,
    expert_ids,
    router,
    gate_weight,
    up_weight,
    down_weight,
):
    n_b, n_h, size = queries.shape
    here = cache_keys.shape[2]
    n_c, n_r, n_e = (lax.axis_size(a) for a in ("ctx", "rows", "expert"))
    rows = n_b * n_h
    struct = jax.ShapeDtypeStruct
    q = queries.transpose(1, 0, 2).reshape(rows, size)
    keys = cache_keys.reshape(n_b, here, size)
    values = cache_values.reshape(n_b, here, size)

    def swap(x, axes):
        return lax.all_to_all(x, axes, split_axis=0, concat_axis=0, tiled=True)

    dims = size * n_b // n_c
    sent = call(
        functools.partial(score_kernel, n_h), struct((n_c, dims + 8, here), BF16),
        keys, q, lengths, values, specs=[HBM] * 4, out_spec=HBM,
        scratch=[
            pltpu.VMEM((n_c, dims + 8, here), BF16), pltpu.VMEM(keys.shape, BF16), pltpu.VMEM(q.shape, BF16),
            pltpu.SMEM((n_b,), jnp.int32), pltpu.VMEM(values.shape, BF16),
            pltpu.SemaphoreType.DMA((4,)), pltpu.SemaphoreType.DMA((n_b,)),
        ],
        limit=60 << 20,
    )
    got = swap(sent, "ctx")
    sent = call(
        functools.partial(attend_kernel, n_h, n_c // n_b), struct((n_c, -(-n_h * n_b // n_c), size), BF16), got, residual,
        specs=[VMEM, VMEM],
    )
    got = swap(sent, "ctx")
    hidden, sent = call(
        hidden_kernel, (struct((rows, size), BF16), struct((n_r * n_e, rows, size), BF16)), got, specs=[VMEM],
    )
    got = swap(sent, ("rows", "expert")).reshape(n_r, n_e * rows, size)
    sent, share = call(
        expert_kernel, (struct((n_r, n_e, rows, size), BF16), struct((rows, n_e), F32)),
        expert_ids.T, got, router.T, gate_weight[0], up_weight[0], down_weight[0],
        specs=[VMEM] * 6,
        scratch=[
            pltpu.VMEM((n_e * n_b, n_e), F32)],
    )
    got = swap(sent.reshape(n_r * n_e, rows, size), ("rows", "expert"))
    width = n_h * size // n_c
    sent = call(
        functools.partial(split_kernel, width), struct((n_c, n_b // 2, 2 * width), F32),
        got, share, hidden, specs=[VMEM, VMEM, VMEM],
    )
    return call(sum_kernel, struct((n_b, width), BF16), swap(sent, "ctx"), specs=[VMEM])


def solution(mesh):
    placed = (
        P("expert", "rows", None),
        P("expert", "rows", "ctx", None),
        P("expert", "rows", "ctx", None),
        P("expert", "rows"),
        P("expert"),
        P("expert", None),
        P(),
        P("expert", None, ("rows", "ctx")),
        P("expert", None, ("rows", "ctx")),
        P("expert", ("rows", "ctx"), None),
    )
    return jax.shard_map(
        body, mesh=mesh, in_specs=placed, out_specs=P("expert", ("rows", "ctx")), check_vma=False
    )
```
